128 devices in a mesh: site: 16 (over x, y_lo, core), mom: 8 (over y_hi, z).
Axes of the slice: x: 4, y: 4 (y_hi: 2, y_lo: 2; y = y_hi * 2 + y_lo), z: 4, core: 2. Of those that a mesh axis runs over, the one named last changes fastest.
Arguments:
- left_seeds: float32 [8, 2, 512, 1024], P('mom', None, 'site'), may hold values from -6 to 6
- right_seeds: float32 [8, 2, 512, 1024], P('mom', None, 'site'), may hold values from -6 to 6
- site_types: int32 [512, 1024], P('site'), may hold values from 0 to 3
- levels: float32 [4], replicated, may hold values from -1 to 1
Outputs:
- moments: float32 [256, 256], P('mom', 'site')
The draws below stay inside these ranges and needn't reach their ends.
All inputs are finite; a program needn't handle non-finite values.
Results may differ from the reference program's by a relative error of at most 0.00011.
Values sent between devices are 32-bit elements; how exact they have to be, the bound alone decides.
A program may use at most 128 MiB of HBM per device.

```python
import math
import jax
import jax.numpy as jnp
from jax import lax

NY = 1024
MB = 32
NTYPES = 4
MOMENTS = 256
NX = 512
N_MOM = 8


def place_ends(array, own_key, least, top_value):
    extent = array.shape
    index_at = [jax.random.randint(jax.random.fold_in(own_key, axis), (), 0, extent[axis]) for axis in range(len(extent))]
    array = array.at[tuple(index_at)].set(least)
    longest = extent.index(max(extent))
    index_at[longest] = (index_at[longest] + 1) % extent[longest]
    return array.at[tuple(index_at)].set(top_value)


def block_levels(rng, extent, cuts, low, high):
    def one(position, blocks):
        steps = jax.random.uniform(jax.random.fold_in(jax.random.fold_in(rng, 6), position), (blocks,), jnp.float32, low / len(cuts), high / len(cuts))
        return jnp.repeat(jnp.exp(steps), extent[position] // blocks).reshape((-1,) + (1,) * (len(extent) - position - 1))

    level = one(*cuts[0])
    for cut in cuts[1:]:
        level = level * one(*cut)
    return level


def centred(stream_key, dims, width, limit, shards=(), kind=jnp.bfloat16):
    entries = width * jax.random.normal(stream_key, dims, jnp.float32)
    if shards:
        entries = entries * block_levels(stream_key, dims, shards, -0.22, 0.18)
    return jnp.clip(entries, -limit, limit).astype(kind)


def setup_inputs(seed: int = 0) -> dict:
    keys = jax.random.split(jax.random.key(seed), 5)
    return {
        "left_seeds": centred(keys[0], (N_MOM, 2, NX, NY), 1.0, 6.0, ((0, 8), (2, 16)), jnp.float32),
        "right_seeds": centred(keys[1], (N_MOM, 2, NX, NY), 1.0, 6.0, ((0, 8), (2, 16)), jnp.float32),
        "site_types": place_ends(jax.random.randint(keys[2], (NX, NY), 0, NTYPES), jax.random.fold_in(keys[2], 1), 0, NTYPES - 1).astype(jnp.int32),
        "levels": jnp.clip(jax.random.uniform(keys[3], (NTYPES,), jnp.float32, -1.0, 1.0), -1.0, 1.0),
    }


SCALE = 1.0 / 4.2

def hamilton(field, energy, parity):
    above = jnp.concatenate([field[..., 1:, :], jnp.zeros_like(field[..., :1, :])], axis=-2)
    below = jnp.concatenate([jnp.zeros_like(field[..., :1, :]), field[..., :-1, :]], axis=-2)
    across = jnp.where(parity, jnp.roll(field, -1, axis=-1), jnp.roll(field, 1, axis=-1))
    return (energy * field + above + below + across) * SCALE

def reference(left_seeds, right_seeds, site_types, levels):
    energy = levels[site_types]
    parity = (jnp.arange(NX)[:, None] + jnp.arange(NY)[None, :]) % 2 == 0

    def chain(opening):

        def step(carry, unused):
            before, current = carry
            fresh = 2.0 * hamilton(current, energy, parity) - before
            return ((current, fresh), fresh)
        _, rest = lax.scan(step, (opening[0], opening[1]), None, length=MB - 2)
        return jnp.concatenate([opening, rest], axis=0)
    left = lax.map(chain, left_seeds).reshape(MOMENTS, NX * NY)
    cheb = lax.map(chain, right_seeds).reshape(MOMENTS, NX, NY)
    above = jnp.concatenate([cheb[:, 1:, :], jnp.zeros_like(cheb[:, :1, :])], axis=1)
    below = jnp.concatenate([jnp.zeros_like(cheb[:, :1, :]), cheb[:, :-1, :]], axis=1)
    right = (above - below).reshape(MOMENTS, NX * NY)
    gram = jnp.dot(left, right.T, precision=lax.Precision.HIGHEST, preferred_element_type=jnp.float32)
    return gram * (1.0 / math.sqrt(NX * NY))
```

```python
import functools
import math

import jax
import jax.numpy as jnp
from jax import lax
from jax.experimental import pallas as pl
from jax.experimental.pallas import tpu as pltpu
from jax.sharding import PartitionSpec as P

MB = 32
HOP = 2.0 / 4.2
MESH = pl.DeviceIdType.MESH
F32 = jnp.float32
BF16 = jnp.bfloat16
LANES = 128
EDGE = 16
GROUP = 4
PAD = 4


def snake(b):
    return jnp.where(b < 4, b, 11 - b)


def spread_kernel(left_ref, right_ref, types_ref, xbuf, ybuf, tbuf, pack,
                  a_send, a_recv, own_sem, x_send, x_recv, y_send, y_recv, t_send, t_recv, t_own):
    t = lax.axis_index("site")
    b = lax.axis_index("mom")
    c = snake(b)
    tiles = 16
    has_low = t > 0
    has_high = t < tiles - 1
    mom_right = snake(lax.rem(c + 1, 8))
    mom_left = snake(lax.rem(c + 7, 8))
    barrier = pltpu.get_barrier_semaphore()
    for j in range(1, 8):
        pl.semaphore_signal(barrier, inc=1, device_id=(t, lax.rem(b + j, 8)), device_id_type=MESH)
    for there, dt in ((has_low, -1), (has_high, 1)):
        @pl.when(there)
        def _():
            for q in (b, mom_left, mom_right):
                pl.semaphore_signal(barrier, inc=1, device_id=(t + dt, q), device_id_type=MESH)
    count = 7 + jnp.where(has_low, 3, 0) + jnp.where(has_high, 3, 0)
    pl.semaphore_wait(barrier, count)

    refs = (left_ref, right_ref)

    def a_copy(lr, j):
        q = lax.rem(b + j, 8)
        col = pl.multiple_of(snake(q) * LANES, LANES)
        return pltpu.make_async_remote_copy(
            src_ref=refs[lr].at[0, :, :, pl.ds(col, LANES)],
            dst_ref=xbuf.at[1, lr, b],
            send_sem=a_send.at[lr, j], recv_sem=a_recv.at[lr, j],
            device_id=(t, q), device_id_type=MESH)

    def a_arrival(lr, j):
        q = lax.rem(b + 8 - j, 8)
        return q, pltpu.make_async_remote_copy(
            src_ref=xbuf.at[1, lr, q], dst_ref=xbuf.at[1, lr, q],
            send_sem=a_send.at[lr, j], recv_sem=a_recv.at[lr, j],
            device_id=(t, q), device_id_type=MESH)

    def own_copy(lr):
        col = pl.multiple_of(c * LANES, LANES)
        return pltpu.make_async_copy(
            refs[lr].at[0, :, :, pl.ds(col, LANES)], xbuf.at[1, lr, b], own_sem.at[lr])

    def t_copy(n, side):
        dt = 1 - 2 * side
        col = pl.multiple_of(lax.rem(c + 7 + n, 8) * LANES, LANES)
        return pltpu.make_async_remote_copy(
            src_ref=types_ref.at[:, pl.ds(col, LANES)], dst_ref=tbuf.at[2 * side, n],
            send_sem=t_send.at[side, n], recv_sem=t_recv.at[side, n],
            device_id=(t + dt, b), device_id_type=MESH)

    def t_keep(n):
        col = pl.multiple_of(lax.rem(c + 7 + n, 8) * LANES, LANES)
        return pltpu.make_async_copy(types_ref.at[:, pl.ds(col, LANES)], tbuf.at[1, n], t_own.at[n])

    for lr in range(2):
        for j in range(1, 8):
            a_copy(lr, j).start()
        own_copy(lr).start()
    for n in range(3):
        t_keep(n).start()

    goes = (has_high, has_low)
    comes = (has_low, has_high)

    def x_copy(lr, j, side):
        q = lax.rem(b + 8 - j, 8)
        return pltpu.make_async_remote_copy(
            src_ref=xbuf.at[1, lr, q], dst_ref=xbuf.at[2 * side, lr, q],
            send_sem=x_send.at[lr, side, j], recv_sem=x_recv.at[lr, side, j],
            device_id=(t + 1 - 2 * side, b), device_id_type=MESH)

    def y_copy(lr, way, dt):
        q = mom_left if way else mom_right
        slot = 1 - dt
        return pltpu.make_async_remote_copy(
            src_ref=pack.at[lr, way], dst_ref=ybuf.at[slot, lr, way],
            send_sem=y_send.at[lr, way, slot], recv_sem=y_recv.at[lr, way, slot],
            device_id=(t + dt, q), device_id_type=MESH)

    lane = lax.broadcasted_iota(jnp.int32, (8, LANES), 1)
    for lr in range(2):
        for j in range(8):
            if j == 0:
                q = b
                own_copy(lr).wait()
            else:
                q, arrival = a_arrival(lr, j)
                arrival.wait_recv()
            for side in range(2):
                @pl.when(goes[side])
                def _():
                    x_copy(lr, j, side).start()
            for way in range(2):
                out = None
                for f in range(2):
                    for g in range(4):
                        slot = f * 4 + g
                        v = xbuf[1, lr, q, f, 8 * g:8 * g + 8, :]
                        source = 0 if way else LANES - EDGE
                        shift = (EDGE * slot - source) % LANES
                        v = pltpu.roll(v, shift, 1) if shift else v
                        out = v if out is None else jnp.where(lane >= EDGE * slot, v, out)
                pack[lr, way, q] = out
        for way in range(2):
            y_copy(lr, way, 0).start()
            @pl.when(has_high)
            def _():
                y_copy(lr, way, 1).start()
            @pl.when(has_low)
            def _():
                y_copy(lr, way, -1).start()
    for side in range(2):
        @pl.when(goes[side])
        def _():
            for n in range(3):
                t_copy(n, side).start()

    for n in range(3):
        t_keep(n).wait()
    for lr in range(2):
        for j in range(1, 8):
            a_copy(lr, j).wait_send()
        for way in range(2):
            y_copy(lr, way, 0).wait()
    for side in range(2):
        dt = 1 - 2 * side
        @pl.when(goes[side])
        def _():
            for n in range(3):
                t_copy(n, side).wait_send()
            for lr in range(2):
                for j in range(8):
                    x_copy(lr, j, side).wait_send()
                for way in range(2):
                    y_copy(lr, way, dt).wait_send()
        @pl.when(comes[side])
        def _():
            for n in range(3):
                t_copy(n, side).wait_recv()
            for lr in range(2):
                for j in range(8):
                    x_copy(lr, j, side).wait_recv()
                for way in range(2):
                    y_copy(lr, way, dt).wait_recv()


def spread(left_seeds, right_seeds, site_types):
    dma = pltpu.SemaphoreType.DMA
    return pl.pallas_call(
        spread_kernel,
        out_shape=(
            jax.ShapeDtypeStruct((3, 2, 8, 2, 32, LANES), F32),
            jax.ShapeDtypeStruct((3, 2, 2, 8, 8, LANES), F32),
            jax.ShapeDtypeStruct((3, 3, 32, LANES), jnp.int32),
        ),
        in_specs=[pl.BlockSpec(memory_space=pltpu.VMEM)] * 3,
        out_specs=[pl.BlockSpec(memory_space=pltpu.VMEM)] * 3,
        scratch_shapes=[
            pltpu.VMEM((2, 2, 8, 8, LANES), F32),
            dma((2, 8)), dma((2, 8)), dma((2,)),
            dma((2, 2, 8)), dma((2, 2, 8)),
            dma((2, 2, 3)), dma((2, 2, 3)),
            dma((2, 3)), dma((2, 3)), dma((3,)),
        ],
        compiler_params=pltpu.CompilerParams(
            collective_id=0, has_side_effects=True, vmem_limit_bytes=32 << 20),
    )(left_seeds, right_seeds, site_types)


def chain_kernel(xbuf, ybuf, tbuf, levels, out, state, energy, arch):
    t = lax.axis_index("site")
    lane = lax.broadcasted_iota(jnp.int32, (8, LANES), 1)
    first_tile = t == 0
    last_tile = t == 15

    lane1 = lax.broadcasted_iota(jnp.int32, (32, LANES), 1)
    for tile in range(3):
        for v in range(2):
            kinds = tbuf[tile, 1] if v == 0 else jnp.where(lane1 < 64, tbuf[tile, 2], tbuf[tile, 0])
            value = jnp.zeros((32, LANES), F32)
            for kind in range(4):
                value = jnp.where(kinds == kind, levels[kind] * HOP, value)
            for r in range(32):
                energy[PAD + 32 * tile + r, v] = jnp.broadcast_to(value[r:r + 1, :], (8, LANES))

    for lr in range(2):
        for tile in range(3):
            xs = xbuf.at[tile, lr].reshape(8 * 2 * 32, LANES)
            y0 = ybuf.at[tile, lr, 0].reshape(64, LANES)
            y1 = ybuf.at[tile, lr, 1].reshape(64, LANES)

            def fill(r, unused):
                low = y0[pl.ds(r, 8, stride=8), :]
                high = y1[pl.ds(r, 8, stride=8), :]
                for f in range(2):
                    for g in range(4):
                        slot = f * 4 + g
                        row = PAD + 32 * tile + 8 * g + r
                        state[lr, f, row, 0] = xs[pl.ds(f * 32 + 8 * g + r, 8, stride=64), :]
                        back = (-EDGE * slot) % LANES
                        left = (LANES - EDGE - EDGE * slot) % LANES
                        h = pltpu.roll(high, back, 1) if back else high
                        l = pltpu.roll(low, left, 1) if left else low
                        state[lr, f, row, 1] = jnp.where(lane < 64, h, l)
                return unused

            lax.fori_loop(0, 8, fill, 0)

    def seal(p):
        for outside, row in ((first_tile, PAD + 31), (last_tile, PAD + 64)):
            @pl.when(outside)
            def _():
                for lr in range(2):
                    for v in range(2):
                        state[lr, p, row, v] = jnp.zeros((8, LANES), F32)

    seal(0)
    seal(1)

    swap_even = lane ^ 1
    swap_odd = (((lane - 1) ^ 1) + 1) & (LANES - 1)
    rim = (lane == 0) | (lane == LANES - 1)

    def pick(x, index):
        return jnp.take_along_axis(x, index, axis=1, mode="promise_in_bounds")

    def rows(start, p, k, keep):
        for lr in range(2):
            above = [[state[lr, p, start + i, v] for v in range(2)] for i in range(-1, GROUP + 1)]
            for i in range(GROUP):
                here = above[i + 1]
                if i % 2 == 0:
                    across = [pick(here[v], swap_even) for v in range(2)]
                else:
                    g = [pick(here[v], swap_odd) for v in range(2)]
                    across = [jnp.where(rim, g[1 - v], g[v]) for v in range(2)]
                for v in range(2):
                    up, down = above[i + 2][v], above[i][v]
                    old = state[lr, 1 - p, start + i, v]
                    new = energy[start + i, v] * here[v] + (up + down + across[v]) * HOP - old
                    state[lr, 1 - p, start + i, v] = new
                if keep:
                    mine = above[i + 2][0] - above[i][0] if lr else here[0]
                    arch[lr, start + i - PAD - 32, pl.ds(pl.multiple_of(8 * k, 8), 8), :] = mine

    def step(k, p):
        low = k // GROUP
        high = (96 - k + GROUP - 1) // GROUP

        def body(keep):
            def run(i, unused):
                rows(pl.multiple_of(PAD + GROUP * i, GROUP), p, k, keep)
                return unused
            return run

        lax.fori_loop(low, 32 // GROUP, body(False), 0)
        lax.fori_loop(32 // GROUP, 64 // GROUP, body(True), 0)
        lax.fori_loop(64 // GROUP, high, body(False), 0)
        seal(1 - p)

    def save(k, p):
        def run(r, unused):
            arch[0, r, pl.ds(8 * k, 8), :] = state[0, p, PAD + 32 + r, 0]
            arch[1, r, pl.ds(8 * k, 8), :] = state[1, p, PAD + 33 + r, 0] - state[1, p, PAD + 31 + r, 0]
            return unused
        lax.fori_loop(0, 32, run, 0, unroll=4)

    save(0, 0)

    def double(i, unused):
        step(2 * i + 1, 1)
        step(2 * i + 2, 0)
        return unused

    lax.fori_loop(0, 15, double, 0)
    save(31, 1)

    out[...] = jnp.zeros_like(out)

    def halves(lr, r):
        x = jnp.concatenate(
            [jnp.concatenate([arch[lr, r + i, pl.ds(q, 32, stride=8), :] for q in range(8)], axis=0)
             for i in range(2)], axis=1)
        high = x.astype(BF16)
        return high, (x - high.astype(F32)).astype(BF16)

    def product(a, c):
        return lax.dot_general(a, c, (((1,), (1,)), ((), ())), preferred_element_type=F32)

    def gram(i, unused):
        lh, ll = halves(0, 2 * i)
        rh, rl = halves(1, 2 * i)
        out[...] += product(rh, lh) + product(rh, ll) + product(rl, lh)
        return unused

    lax.fori_loop(0, 16, gram, 0)


def chain(xbuf, ybuf, tbuf, levels):
    return pl.pallas_call(
        chain_kernel,
        out_shape=jax.ShapeDtypeStruct((256, 256), F32),
        in_specs=[pl.BlockSpec(memory_space=pltpu.VMEM)] * 3 + [pl.BlockSpec(memory_space=pltpu.SMEM)],
        out_specs=pl.BlockSpec(memory_space=pltpu.VMEM),
        scratch_shapes=[
            pltpu.VMEM((2, 2, 96 + 2 * PAD, 2, 8, LANES), F32),
            pltpu.VMEM((96 + 2 * PAD, 2, 8, LANES), F32),
            pltpu.VMEM((2, 32, 256, LANES), F32),
        ],
        compiler_params=pltpu.CompilerParams(vmem_limit_bytes=48 << 20),
    )(xbuf, ybuf, tbuf, levels)


def reduce_kernel(scale, sums, out, got, turned, parts, s_send, s_recv, m_send, m_recv):
    t = lax.axis_index("site")
    b = lax.axis_index("mom")
    barrier = pltpu.get_barrier_semaphore()
    for j in range(1, 16):
        pl.semaphore_signal(barrier, inc=1, device_id=(lax.rem(t + j, 16), b), device_id_type=MESH)
    for j in range(1, 8):
        pl.semaphore_signal(barrier, inc=1, device_id=(t, lax.rem(b + j, 8)), device_id_type=MESH)
    pl.semaphore_wait(barrier, 22)

    def s_copy(j):
        s = lax.rem(t + j, 16)
        return pltpu.make_async_remote_copy(
            src_ref=sums.at[pl.ds(pl.multiple_of(16 * s, 16), 16), :], dst_ref=got.at[j],
            send_sem=s_send.at[j], recv_sem=s_recv.at[j], device_id=(s, b), device_id_type=MESH)

    for j in range(1, 16):
        s_copy(j).start()
    total = sums[pl.ds(pl.multiple_of(16 * t, 16), 16), :]
    for j in range(1, 16):
        s_copy(j).wait_recv()
        total = total + got[j]
    turned[:, 0:16] = jnp.transpose(total * scale)

    def m_copy(j):
        q = lax.rem(b + j, 8)
        return pltpu.make_async_remote_copy(
            src_ref=turned.at[pl.ds(pl.multiple_of(32 * q, 32), 32), :], dst_ref=parts.at[j],
            send_sem=m_send.at[j], recv_sem=m_recv.at[j], device_id=(t, q), device_id_type=MESH)

    for j in range(1, 8):
        m_copy(j).start()
    final = turned[pl.ds(pl.multiple_of(32 * b, 32), 32), :]
    for j in range(1, 8):
        m_copy(j).wait_recv()
        final = final + parts[j]
    out[...] = final[:, 0:16]
    for j in range(1, 16):
        s_copy(j).wait_send()
    for j in range(1, 8):
        m_copy(j).wait_send()


def reduce(sums, scale):
    dma = pltpu.SemaphoreType.DMA
    return pl.pallas_call(
        functools.partial(reduce_kernel, scale),
        out_shape=jax.ShapeDtypeStruct((32, 16), F32),
        in_specs=[pl.BlockSpec(memory_space=pltpu.VMEM)],
        out_specs=pl.BlockSpec(memory_space=pltpu.VMEM),
        scratch_shapes=[
            pltpu.VMEM((16, 16, 256), F32),
            pltpu.VMEM((256, LANES), F32),
            pltpu.VMEM((8, 32, LANES), F32),
            dma((16,)), dma((16,)), dma((8,)), dma((8,)),
        ],
        compiler_params=pltpu.CompilerParams(collective_id=1, has_side_effects=True),
    )(sums)


def on_device(left_seeds, right_seeds, site_types, levels):
    xbuf, ybuf, tbuf = spread(left_seeds, right_seeds, site_types)
    sums = chain(xbuf, ybuf, tbuf, levels)
    return reduce(sums, 1.0 / math.sqrt(512 * 1024))


def solution(mesh):
    return jax.shard_map(
        on_device,
        mesh=mesh,
        in_specs=(P("mom", None, "site", None), P("mom", None, "site", None), P("site", None), P()),
        out_specs=P("mom", "site"),
        check_vma=False,
    )
```

```python
import functools
import math

import jax
import jax.numpy as jnp
from jax import lax
from jax.experimental import pallas as pl
from jax.experimental.pallas import tpu as pltpu
from jax.sharding import PartitionSpec as P

MB = 32
HOP = 2.0 / 4.2
MESH = pl.DeviceIdType.MESH
F32 = jnp.float32
BF16 = jnp.bfloat16
LANES = 128
HALF = 64
EDGE = 8
PAD = 4
PHASES = 5


def snake(b):
    return jnp.where(b < 4, b, 11 - b)


def lanes_of(rows):
    return lax.broadcasted_iota(jnp.int32, (rows, LANES), 1)


def pieces(x):
    high = x.astype(BF16)
    rest = x - high.astype(F32)
    middle = rest.astype(BF16)
    low = (rest - middle.astype(F32)).astype(BF16)
    return jnp.concatenate([high, middle, low], axis=1)


def unzip(x):
    row = lax.broadcasted_iota(jnp.int32, (3 * LANES, LANES), 0) % LANES
    col = lax.broadcasted_iota(jnp.int32, (3 * LANES, LANES), 1)
    source = jnp.where(col < HALF, 2 * col, 2 * (col - HALF) + 1)
    matrix = jnp.where(row == source, 1.0, 0.0).astype(BF16)
    return jnp.dot(pieces(x), matrix, preferred_element_type=F32)


def spread_energy(ebuf, energy):
    lane = lanes_of(32)
    for tile in range(3):
        own = ebuf[tile, 1]
        halo = jnp.where(lane % HALF < 32, pltpu.roll(ebuf[tile, 2], HALF, 1), pltpu.roll(ebuf[tile, 0], HALF, 1))
        for v in range(2):
            value = jnp.where(lane < HALF, own, halo) if v == 0 else jnp.where(lane < HALF, halo, own)
            for r in range(32):
                energy[PAD + 32 * tile + r, v] = jnp.broadcast_to(value[r:r + 1, :], (8, LANES))


def fill(lr, t, xbuf, ybuf, state):
    lane = lanes_of(8)
    inner = lane < HALF
    for tile in range(3):
        xs = xbuf.at[tile, lr].reshape(8 * 2 * 32, LANES)
        y0 = ybuf.at[tile, lr, 0].reshape(64, LANES)
        y1 = ybuf.at[tile, lr, 1].reshape(64, LANES)
        for r in range(8):
            low = y0[pl.ds(r, 8, stride=8), :]
            high = y1[pl.ds(r, 8, stride=8), :]
            for f in range(2):
                for g in range(4):
                    slot = f * 4 + g
                    row = 32 * tile + 8 * g + r
                    own = xs[pl.ds(f * 32 + 8 * g + r, 8, stride=64), :]
                    halo = jnp.where(
                        lane % HALF < 32,
                        pltpu.roll(high, HALF - EDGE * slot, 1),
                        pltpu.roll(low, LANES - EDGE - EDGE * slot, 1))
                    pair = (jnp.where(inner, own, halo), jnp.where(inner, halo, own))
                    for v in range(2):
                        new = pair[v]
                        if row == 31:
                            new = jnp.where(t == 0, 0.0, new)
                        if row == 64:
                            new = jnp.where(t == 15, 0.0, new)
                        state[f, PAD + row, v] = new


def step(lr, t, k, p, low, high, state, energy, arch):
    lane = lanes_of(8)
    load = lambda row: [state[p, PAD + row, v] for v in range(2)]
    below, here = load(low - 1), load(low)
    for row in range(low, high):
        above = load(row + 1)
        turn = (HALF, HALF) if row % 2 == 0 else (HALF + 1, HALF - 1)
        for v in range(2):
            across = pltpu.roll(here[1 - v], turn[v], 1)
            new = (energy[PAD + row, v] * here[v]
                   + (above[v] + below[v] + across) * HOP - state[1 - p, PAD + row, v])
            if row == 31:
                new = jnp.where(t == 0, 0.0, new)
            if row == 64:
                new = jnp.where(t == 15, 0.0, new)
            state[1 - p, PAD + row, v] = new
        if 32 <= row < 64:
            keep(lr, lane, row, k, below, here, above, arch)
        below, here = here, above


def keep(lr, lane, row, k, below, here, above, arch):
    join = lambda x: jnp.where(lane < HALF, x[0], x[1])
    mine = join(above) - join(below) if lr else join(here)
    arch[lr, row - 32, pl.ds(pl.multiple_of(8 * k, 8), 8), :] = mine


def save(lr, k, p, state, arch):
    lane = lanes_of(8)
    for row in range(32, 64):
        load = lambda i: [state[p, PAD + row + i, v] for v in range(2)]
        keep(lr, lane, row, k, load(-1), load(0), load(1), arch)


def run(lr, t, state, energy, arch):
    save(lr, 0, 0, state, arch)
    pairs = 15 // PHASES
    for phase in range(PHASES):
        first = 2 * pairs * phase

        def double(i, unused):
            k = first + 2 * i + 1
            step(lr, t, k, 1, first + 1, 95 - first, state, energy, arch)
            step(lr, t, k + 1, 0, first + 2, 94 - first, state, energy, arch)
            return unused

        lax.fori_loop(0, pairs, double, 0)
    save(lr, 31, 1, state, arch)


def gram(arch, sums):
    sums[...] = jnp.zeros_like(sums)

    def halves(lr, r):
        x = jnp.concatenate(
            [jnp.concatenate([arch[lr, r + i, pl.ds(q, 32, stride=8), :] for q in range(8)], axis=0)
             for i in range(2)], axis=1)
        high = x.astype(BF16)
        return high, (x - high.astype(F32)).astype(BF16)

    def product(a, c):
        return lax.dot_general(a, c, (((1,), (1,)), ((), ())), preferred_element_type=F32)

    def add(i, unused):
        lh, ll = halves(0, 2 * i)
        rh, rl = halves(1, 2 * i)
        sums[...] += product(rh, lh) + product(rh, ll) + product(rl, lh)
        return unused

    lax.fori_loop(0, 16, add, 0)


def kernel(scale, left_ref, right_ref, types_ref, levels, out,
           raw, types, seeds, xbuf, ybuf, ebuf, pack, state, energy, arch, sums, got, turned, parts,
           in_sem, a_send, a_recv, own_sem, x_send, x_recv, y_send, y_recv, e_send, e_recv,
           s_send, s_recv, m_send, m_recv):
    t = lax.axis_index("site")
    b = lax.axis_index("mom")
    c = snake(b)
    has_low = t > 0
    has_high = t < 15
    mom_right = snake(lax.rem(c + 1, 8))
    mom_left = snake(lax.rem(c + 7, 8))

    loads = [pltpu.make_async_copy(left_ref.at[0], raw.at[0], in_sem.at[0]),
             pltpu.make_async_copy(right_ref.at[0], raw.at[1], in_sem.at[1]),
             pltpu.make_async_copy(types_ref, types, in_sem.at[2])]
    for load in loads:
        load.start()

    barrier = pltpu.get_barrier_semaphore()
    for j in range(1, 8):
        pl.semaphore_signal(barrier, inc=1, device_id=(t, lax.rem(b + j, 8)), device_id_type=MESH)
    for j in range(1, 16):
        pl.semaphore_signal(barrier, inc=1, device_id=(lax.rem(t + j, 16), b), device_id_type=MESH)
    for there, dt in ((has_low, -1), (has_high, 1)):
        @pl.when(there)
        def _():
            for q in (mom_left, mom_right):
                pl.semaphore_signal(barrier, inc=1, device_id=(t + dt, q), device_id_type=MESH)

    def unzip_seeds(lr):
        x = jnp.concatenate(
            [raw[lr, :, :, LANES * i:LANES * i + LANES].reshape(64, LANES) for i in range(8)], axis=0)
        seeds[lr] = unzip(x).reshape(8, 2, 32, LANES)

    loads[0].wait()
    unzip_seeds(0)
    pl.semaphore_wait(barrier, 22 + jnp.where(has_low, 2, 0) + jnp.where(has_high, 2, 0))

    def a_copy(lr, j):
        q = lax.rem(b + j, 8)
        return pltpu.make_async_remote_copy(
            src_ref=seeds.at[lr, snake(q)], dst_ref=xbuf.at[1, lr, b],
            send_sem=a_send.at[lr, j], recv_sem=a_recv.at[lr, j],
            device_id=(t, q), device_id_type=MESH)

    def a_arrival(lr, j):
        q = lax.rem(b + 8 - j, 8)
        return q, pltpu.make_async_remote_copy(
            src_ref=xbuf.at[1, lr, q], dst_ref=xbuf.at[1, lr, q],
            send_sem=a_send.at[lr, j], recv_sem=a_recv.at[lr, j],
            device_id=(t, q), device_id_type=MESH)

    def own_copy(lr):
        return pltpu.make_async_copy(seeds.at[lr, c], xbuf.at[1, lr, b], own_sem.at[lr])

    def a_start(lr):
        for j in range(1, 8):
            a_copy(lr, j).start()
        own_copy(lr).start()

    goes = (has_high, has_low)
    comes = (has_low, has_high)

    def e_copy(side):
        return pltpu.make_async_remote_copy(
            src_ref=ebuf.at[1], dst_ref=ebuf.at[2 * side],
            send_sem=e_send.at[side], recv_sem=e_recv.at[side],
            device_id=(t + 1 - 2 * side, b), device_id_type=MESH)

    def x_copy(lr, j, side):
        q = lax.rem(b + 8 - j, 8)
        return pltpu.make_async_remote_copy(
            src_ref=xbuf.at[1, lr, q], dst_ref=xbuf.at[2 * side, lr, q],
            send_sem=x_send.at[lr, side, j], recv_sem=x_recv.at[lr, side, j],
            device_id=(t + 1 - 2 * side, b), device_id_type=MESH)

    def y_copy(lr, way, dt):
        q = mom_left if way else mom_right
        slot = 1 - dt
        return pltpu.make_async_remote_copy(
            src_ref=pack.at[lr, way], dst_ref=ybuf.at[slot, lr, way],
            send_sem=y_send.at[lr, way, slot], recv_sem=y_recv.at[lr, way, slot],
            device_id=(t + dt, q), device_id_type=MESH)

    a_start(0)
    loads[1].wait()
    unzip_seeds(1)
    a_start(1)

    loads[2].wait()
    values = []
    for n in range(3):
        col = pl.multiple_of(lax.rem(c + 7 + n, 8) * LANES, LANES)
        kinds = types[:, pl.ds(col, LANES)]
        value = jnp.zeros((32, LANES), F32)
        for kind in range(4):
            value = jnp.where(kinds == kind, levels[kind] * HOP, value)
        values.append(value)
    ebuf[1] = unzip(jnp.concatenate(values, axis=0)).reshape(3, 32, LANES)
    for side in range(2):
        @pl.when(goes[side])
        def _():
            e_copy(side).start()

    lane = lanes_of(8)

    def forward(lr):
        for j in range(8):
            if j == 0:
                q = b
                own_copy(lr).wait()
            else:
                q, arrival = a_arrival(lr, j)
                arrival.wait_recv()
            for side in range(2):
                @pl.when(goes[side])
                def _():
                    x_copy(lr, j, side).start()
            for way in range(2):
                packed = None
                for f in range(2):
                    for g in range(4):
                        slot = f * 4 + g
                        v = xbuf[1, lr, q, f, 8 * g:8 * g + 8, :]
                        source = 0 if way else HALF - EDGE
                        v = pltpu.roll(v, (EDGE * slot - source) % LANES, 1) if EDGE * slot != source else v
                        packed = v if packed is None else jnp.where(lane % HALF >= EDGE * slot, v, packed)
                pack[lr, way, q] = packed
        for way in range(2):
            y_copy(lr, way, 0).start()
            for side in range(2):
                @pl.when(goes[side])
                def _():
                    y_copy(lr, way, 1 - 2 * side).start()

    forward(0)
    forward(1)

    for side in range(2):
        @pl.when(comes[side])
        def _():
            e_copy(side).wait_recv()
    spread_energy(ebuf, energy)

    for lr in range(2):
        for way in range(2):
            y_copy(lr, way, 0).wait_recv()
        for side in range(2):
            @pl.when(comes[side])
            def _():
                for j in range(8):
                    x_copy(lr, j, side).wait_recv()
                for way in range(2):
                    y_copy(lr, way, 1 - 2 * side).wait_recv()
        fill(lr, t, xbuf, ybuf, state)
        run(lr, t, state, energy, arch)

    gram(arch, sums)

    def s_copy(j):
        s = lax.rem(t + j, 16)
        return pltpu.make_async_remote_copy(
            src_ref=sums.at[pl.ds(pl.multiple_of(16 * s, 16), 16), :], dst_ref=got.at[j],
            send_sem=s_send.at[j], recv_sem=s_recv.at[j], device_id=(s, b), device_id_type=MESH)

    for j in range(1, 16):
        s_copy(j).start()
    total = sums[pl.ds(pl.multiple_of(16 * t, 16), 16), :]
    for j in range(1, 16):
        s_copy(j).wait_recv()
        total = total + got[j]
    turned[:, 0:16] = jnp.transpose(total * scale)

    def m_copy(j):
        q = lax.rem(b + j, 8)
        return pltpu.make_async_remote_copy(
            src_ref=turned.at[pl.ds(pl.multiple_of(32 * q, 32), 32), :], dst_ref=parts.at[j],
            send_sem=m_send.at[j], recv_sem=m_recv.at[j], device_id=(t, q), device_id_type=MESH)

    for j in range(1, 8):
        m_copy(j).start()
    final = turned[pl.ds(pl.multiple_of(32 * b, 32), 32), :]
    for j in range(1, 8):
        m_copy(j).wait_recv()
        final = final + parts[j]
    out[...] = final[:, 0:16]

    for j in range(1, 16):
        s_copy(j).wait_send()
    for j in range(1, 8):
        m_copy(j).wait_send()
    for lr in range(2):
        for j in range(1, 8):
            a_copy(lr, j).wait_send()
        for way in range(2):
            y_copy(lr, way, 0).wait_send()
    for side in range(2):
        @pl.when(goes[side])
        def _():
            e_copy(side).wait_send()
            for lr in range(2):
                for j in range(8):
                    x_copy(lr, j, side).wait_send()
                for way in range(2):
                    y_copy(lr, way, 1 - 2 * side).wait_send()


def on_device(left_seeds, right_seeds, site_types, levels):
    dma = pltpu.SemaphoreType.DMA
    return pl.pallas_call(
        functools.partial(kernel, 1.0 / math.sqrt(512 * 1024)),
        out_shape=jax.ShapeDtypeStruct((32, 16), F32),
        in_specs=[pl.BlockSpec(memory_space=pl.ANY)] * 3 + [pl.BlockSpec(memory_space=pltpu.SMEM)],
        out_specs=pl.BlockSpec(memory_space=pltpu.VMEM),
        scratch_shapes=[
            pltpu.VMEM((2, 2, 32, 1024), F32),
            pltpu.VMEM((32, 1024), jnp.int32),
            pltpu.VMEM((2, 8, 2, 32, LANES), F32),
            pltpu.VMEM((3, 2, 8, 2, 32, LANES), F32),
            pltpu.VMEM((3, 2, 2, 8, 8, LANES), F32),
            pltpu.VMEM((3, 3, 32, LANES), F32),
            pltpu.VMEM((2, 2, 8, 8, LANES), F32),
            pltpu.VMEM((2, 96 + 2 * PAD, 2, 8, LANES), F32),
            pltpu.VMEM((96 + 2 * PAD, 2, 8, LANES), F32),
            pltpu.VMEM((2, 32, 256, LANES), F32),
            pltpu.VMEM((256, 256), F32),
            pltpu.VMEM((16, 16, 256), F32),
            pltpu.VMEM((256, LANES), F32),
            pltpu.VMEM((8, 32, LANES), F32),
            dma((3,)),
            dma((2, 8)), dma((2, 8)), dma((2,)),
            dma((2, 2, 8)), dma((2, 2, 8)),
            dma((2, 2, 3)), dma((2, 2, 3)),
            dma((2,)), dma((2,)),
            dma((16,)), dma((16,)), dma((8,)), dma((8,)),
        ],
        compiler_params=pltpu.CompilerParams(
            collective_id=0, has_side_effects=True, vmem_limit_bytes=48 << 20),
    )(left_seeds, right_seeds, site_types, levels)


def solution(mesh):
    return jax.shard_map(
        on_device,
        mesh=mesh,
        in_specs=(P("mom", None, "site", None), P("mom", None, "site", None), P("site", None), P()),
        out_specs=P("mom", "site"),
        check_vma=False,
    )
```

```python
import functools
import math

import jax
import jax.numpy as jnp
from jax import lax
from jax.experimental import pallas as pl
from jax.experimental.pallas import tpu as pltpu
from jax.sharding import PartitionSpec as P

MB = 32
HOP = 2.0 / 4.2
MESH = pl.DeviceIdType.MESH
F32 = jnp.float32
BF16 = jnp.bfloat16
LANES = 128
HALF = 64
EDGE = 8
PAD = 4
PHASES = 5


def snake(b):
    return jnp.where(b < 4, b, 11 - b)


def place(tile):
    return tile ^ (((tile >> 2) & 1) << 1)


def lanes_of(rows):
    return lax.broadcasted_iota(jnp.int32, (rows, LANES), 1)


def pieces(x):
    high = x.astype(BF16)
    rest = x - high.astype(F32)
    middle = rest.astype(BF16)
    low = (rest - middle.astype(F32)).astype(BF16)
    return jnp.concatenate([high, middle, low], axis=1)


def unzip(x):
    row = lax.broadcasted_iota(jnp.int32, (3 * LANES, LANES), 0) % LANES
    col = lax.broadcasted_iota(jnp.int32, (3 * LANES, LANES), 1)
    source = jnp.where(col < HALF, 2 * col, 2 * (col - HALF) + 1)
    matrix = jnp.where(row == source, 1.0, 0.0).astype(BF16)
    return jnp.dot(pieces(x), matrix, preferred_element_type=F32)


def spread_energy(ebuf, energy):
    lane = lanes_of(32)
    for tile in range(3):
        own = ebuf[tile, 1]
        halo = jnp.where(lane % HALF < 32, pltpu.roll(ebuf[tile, 2], HALF, 1), pltpu.roll(ebuf[tile, 0], HALF, 1))
        for v in range(2):
            value = jnp.where(lane < HALF, own, halo) if v == 0 else jnp.where(lane < HALF, halo, own)
            for r in range(32):
                energy[PAD + 32 * tile + r, v] = jnp.broadcast_to(value[r:r + 1, :], (8, LANES))


def fill(lr, t, xbuf, ybuf, state):
    lane = lanes_of(8)
    inner = lane < HALF
    for tile in range(3):
        xs = xbuf.at[tile, lr].reshape(8 * 2 * 32, LANES)
        y0 = ybuf.at[tile, lr, 0].reshape(64, LANES)
        y1 = ybuf.at[tile, lr, 1].reshape(64, LANES)
        for r in range(8):
            low = y0[pl.ds(r, 8, stride=8), :]
            high = y1[pl.ds(r, 8, stride=8), :]
            for f in range(2):
                for g in range(4):
                    slot = f * 4 + g
                    row = 32 * tile + 8 * g + r
                    own = xs[pl.ds(f * 32 + 8 * g + r, 8, stride=64), :]
                    halo = jnp.where(
                        lane % HALF < 32,
                        pltpu.roll(high, HALF - EDGE * slot, 1),
                        pltpu.roll(low, LANES - EDGE - EDGE * slot, 1))
                    pair = (jnp.where(inner, own, halo), jnp.where(inner, halo, own))
                    for v in range(2):
                        new = pair[v]
                        if row == 31:
                            new = jnp.where(t == 0, 0.0, new)
                        if row == 64:
                            new = jnp.where(t == 15, 0.0, new)
                        state[f, PAD + row, v] = new


def step(lr, t, k, p, low, high, state, energy, arch):
    lane = lanes_of(8)
    load = lambda row: [state[p, PAD + row, v] for v in range(2)]
    below, here = load(low - 1), load(low)
    for row in range(low, high):
        above = load(row + 1)
        turn = (HALF, HALF) if row % 2 == 0 else (HALF + 1, HALF - 1)
        for v in range(2):
            across = pltpu.roll(here[1 - v], turn[v], 1)
            new = (energy[PAD + row, v] * here[v]
                   + (above[v] + below[v] + across) * HOP - state[1 - p, PAD + row, v])
            if row == 31:
                new = jnp.where(t == 0, 0.0, new)
            if row == 64:
                new = jnp.where(t == 15, 0.0, new)
            state[1 - p, PAD + row, v] = new
        if 32 <= row < 64:
            keep(lr, lane, row, k, below, here, above, arch)
        below, here = here, above


def keep(lr, lane, row, k, below, here, above, arch):
    join = lambda x: jnp.where(lane < HALF, x[0], x[1])
    mine = join(above) - join(below) if lr else join(here)
    arch[lr, row - 32, pl.ds(pl.multiple_of(8 * k, 8), 8), :] = mine


def save(lr, k, p, state, arch):
    lane = lanes_of(8)
    for row in range(32, 64):
        load = lambda i: [state[p, PAD + row + i, v] for v in range(2)]
        keep(lr, lane, row, k, load(-1), load(0), load(1), arch)


def run(lr, t, state, energy, arch):
    save(lr, 0, 0, state, arch)
    pairs = 15 // PHASES
    for phase in range(PHASES):
        first = 2 * pairs * phase

        def double(i, unused):
            k = first + 2 * i + 1
            step(lr, t, k, 1, first + 1, 95 - first, state, energy, arch)
            step(lr, t, k + 1, 0, first + 2, 94 - first, state, energy, arch)
            return unused

        lax.fori_loop(0, pairs, double, 0)
    save(lr, 31, 1, state, arch)


def halves(arch, lr, i):
    x = jnp.concatenate(
        [jnp.concatenate([arch[lr, 2 * i + n, pl.ds(q, 32, stride=8), :] for q in range(8)], axis=0)
         for n in range(2)], axis=1)
    high = x.astype(BF16)
    return high, (x - high.astype(F32)).astype(BF16)


def split_left(arch, lefts):
    def one(i, unused):
        lefts[i, 0], lefts[i, 1] = halves(arch, 0, i)
        return unused

    lax.fori_loop(0, 16, one, 0, unroll=2)


def gram(arch, lefts, sums):
    sums[...] = jnp.zeros_like(sums)

    def product(a, c):
        return lax.dot_general(a, c, (((1,), (1,)), ((), ())), preferred_element_type=F32)

    def add(i, unused):
        lh, ll = lefts[i, 0], lefts[i, 1]
        rh, rl = halves(arch, 1, i)
        sums[...] += product(rh, lh) + product(rh, ll) + product(rl, lh)
        return unused

    lax.fori_loop(0, 16, add, 0, unroll=4)


def kernel(scale, left_ref, right_ref, types_ref, levels, out,
           raw, types, seeds, levels_here, xbuf, ybuf, ebuf, pack, state, energy, arch, lefts, sums, got, turned,
           parts,
           in_sem, a_send, a_recv, own_sem, x_send, x_recv, y_send, y_recv, e_send, e_recv,
           s_send, s_recv, m_send, m_recv):
    t = lax.axis_index("site")
    b = lax.axis_index("mom")
    c = snake(b)
    mine = place(t)
    stays = mine == t
    moves = mine != t
    has_low = mine > 0
    has_high = mine < 15
    mom_right = snake(lax.rem(c + 1, 8))
    mom_left = snake(lax.rem(c + 7, 8))

    loads = [pltpu.make_async_copy(left_ref.at[0], raw.at[0], in_sem.at[0]),
             pltpu.make_async_copy(right_ref.at[0], raw.at[1], in_sem.at[1]),
             pltpu.make_async_copy(types_ref, types, in_sem.at[2])]
    for load in loads:
        load.start()

    barrier = pltpu.get_barrier_semaphore()
    for j in range(1, 8):
        pl.semaphore_signal(barrier, inc=1, device_id=(t, lax.rem(b + j, 8)), device_id_type=MESH)
    for j in range(1, 16):
        pl.semaphore_signal(barrier, inc=1, device_id=(lax.rem(t + j, 16), b), device_id_type=MESH)
    for there, dt in ((has_low, -1), (has_high, 1)):
        @pl.when(there)
        def _():
            for q in (mom_left, mom_right):
                pl.semaphore_signal(barrier, inc=1, device_id=(place(mine + dt), q), device_id_type=MESH)

    @pl.when(moves)
    def _():
        for j in range(1, 8):
            pl.semaphore_signal(barrier, inc=1, device_id=(mine, lax.rem(b + j, 8)), device_id_type=MESH)

    def unzip_seeds(lr):
        x = jnp.concatenate(
            [raw[lr, :, :, LANES * i:LANES * i + LANES].reshape(64, LANES) for i in range(8)], axis=0)
        seeds[lr] = unzip(x).reshape(8, 2, 32, LANES)

    loads[0].wait()
    unzip_seeds(0)
    pl.semaphore_wait(
        barrier, 22 + jnp.where(has_low, 2, 0) + jnp.where(has_high, 2, 0) + jnp.where(moves, 7, 0))

    def a_copy(lr, j):
        q = lax.rem(b + j, 8)
        return pltpu.make_async_remote_copy(
            src_ref=seeds.at[lr, snake(q)], dst_ref=xbuf.at[1, lr, b],
            send_sem=a_send.at[lr, j], recv_sem=a_recv.at[lr, j],
            device_id=(mine, q), device_id_type=MESH)

    def a_arrival(lr, j):
        q = lax.rem(b + 8 - j, 8)
        return q, pltpu.make_async_remote_copy(
            src_ref=xbuf.at[1, lr, q], dst_ref=xbuf.at[1, lr, q],
            send_sem=a_send.at[lr, j], recv_sem=a_recv.at[lr, j],
            device_id=(mine, q), device_id_type=MESH)

    def own_copy(lr):
        return pltpu.make_async_copy(seeds.at[lr, c], xbuf.at[1, lr, b], own_sem.at[lr])

    def a_start(lr):
        for j in range(1, 8):
            a_copy(lr, j).start()

        @pl.when(stays)
        def _():
            own_copy(lr).start()

        @pl.when(moves)
        def _():
            a_copy(lr, 0).start()

    goes = (has_high, has_low)
    comes = (has_low, has_high)

    def e_copy(dt):
        return pltpu.make_async_remote_copy(
            src_ref=levels_here, dst_ref=ebuf.at[1 - dt],
            send_sem=e_send.at[1 - dt], recv_sem=e_recv.at[1 - dt],
            device_id=(place(t + dt), b), device_id_type=MESH)

    def e_keep():
        return pltpu.make_async_copy(levels_here, ebuf.at[1], e_send.at[1])

    def x_copy(lr, j, side):
        q = lax.rem(b + 8 - j, 8)
        return pltpu.make_async_remote_copy(
            src_ref=xbuf.at[1, lr, q], dst_ref=xbuf.at[2 * side, lr, q],
            send_sem=x_send.at[lr, side, j], recv_sem=x_recv.at[lr, side, j],
            device_id=(place(mine + 1 - 2 * side), b), device_id_type=MESH)

    def y_copy(lr, way, dt):
        q = mom_left if way else mom_right
        slot = 1 - dt
        return pltpu.make_async_remote_copy(
            src_ref=pack.at[lr, way], dst_ref=ybuf.at[slot, lr, way],
            send_sem=y_send.at[lr, way, slot], recv_sem=y_recv.at[lr, way, slot],
            device_id=(place(mine + dt), q), device_id_type=MESH)

    a_start(0)
    loads[1].wait()
    unzip_seeds(1)
    a_start(1)

    loads[2].wait()
    values = []
    for n in range(3):
        col = pl.multiple_of(lax.rem(c + 7 + n, 8) * LANES, LANES)
        kinds = types[:, pl.ds(col, LANES)]
        value = jnp.zeros((32, LANES), F32)
        for kind in range(4):
            value = jnp.where(kinds == kind, levels[kind] * HOP, value)
        values.append(value)
    levels_here[...] = unzip(jnp.concatenate(values, axis=0)).reshape(3, 32, LANES)

    @pl.when(t < 15)
    def _():
        e_copy(1).start()

    @pl.when(t > 0)
    def _():
        e_copy(-1).start()

    @pl.when(moves)
    def _():
        e_copy(0).start()

    @pl.when(stays)
    def _():
        e_keep().start()

    lane = lanes_of(8)

    def forward(lr):
        for j in range(8):
            if j == 0:
                q = b

                @pl.when(stays)
                def _():
                    own_copy(lr).wait()

                @pl.when(moves)
                def _():
                    a_copy(lr, 0).wait_recv()
            else:
                q, arrival = a_arrival(lr, j)
                arrival.wait_recv()
            for side in range(2):
                @pl.when(goes[side])
                def _():
                    x_copy(lr, j, side).start()
            for way in range(2):
                packed = None
                for f in range(2):
                    for g in range(4):
                        slot = f * 4 + g
                        v = xbuf[1, lr, q, f, 8 * g:8 * g + 8, :]
                        source = 0 if way else HALF - EDGE
                        v = pltpu.roll(v, (EDGE * slot - source) % LANES, 1) if EDGE * slot != source else v
                        packed = v if packed is None else jnp.where(lane % HALF >= EDGE * slot, v, packed)
                pack[lr, way, q] = packed
        for way in range(2):
            y_copy(lr, way, 0).start()
            for side in range(2):
                @pl.when(goes[side])
                def _():
                    y_copy(lr, way, 1 - 2 * side).start()

    forward(0)
    forward(1)

    for side in range(2):
        @pl.when(comes[side])
        def _():
            e_copy(1 - 2 * side).wait_recv()

    @pl.when(moves)
    def _():
        e_copy(0).wait_recv()

    @pl.when(stays)
    def _():
        e_keep().wait()

    spread_energy(ebuf, energy)

    for lr in range(2):
        for way in range(2):
            y_copy(lr, way, 0).wait_recv()
        for side in range(2):
            @pl.when(comes[side])
            def _():
                for j in range(8):
                    x_copy(lr, j, side).wait_recv()
                for way in range(2):
                    y_copy(lr, way, 1 - 2 * side).wait_recv()
        fill(lr, mine, xbuf, ybuf, state)
        run(lr, mine, state, energy, arch)
        if lr == 0:
            split_left(arch, lefts)

    gram(arch, lefts, sums)

    def s_copy(j):
        s = lax.rem(t + j, 16)
        return pltpu.make_async_remote_copy(
            src_ref=sums.at[pl.ds(pl.multiple_of(16 * s, 16), 16), :], dst_ref=got.at[j],
            send_sem=s_send.at[j], recv_sem=s_recv.at[j], device_id=(s, b), device_id_type=MESH)

    for j in range(1, 16):
        s_copy(j).start()
    total = sums[pl.ds(pl.multiple_of(16 * t, 16), 16), :]
    for j in range(1, 16):
        s_copy(j).wait_recv()
        total = total + got[j]
    turned[:, 0:16] = jnp.transpose(total * scale)

    def m_copy(j):
        q = lax.rem(b + j, 8)
        return pltpu.make_async_remote_copy(
            src_ref=turned.at[pl.ds(pl.multiple_of(32 * q, 32), 32), :], dst_ref=parts.at[j],
            send_sem=m_send.at[j], recv_sem=m_recv.at[j], device_id=(t, q), device_id_type=MESH)

    for j in range(1, 8):
        m_copy(j).start()
    final = turned[pl.ds(pl.multiple_of(32 * b, 32), 32), :]
    for j in range(1, 8):
        m_copy(j).wait_recv()
        final = final + parts[j]
    out[...] = final[:, 0:16]

    for j in range(1, 16):
        s_copy(j).wait_send()
    for j in range(1, 8):
        m_copy(j).wait_send()
    for lr in range(2):
        for j in range(1, 8):
            a_copy(lr, j).wait_send()
        for way in range(2):
            y_copy(lr, way, 0).wait_send()

    @pl.when(t < 15)
    def _():
        e_copy(1).wait_send()

    @pl.when(t > 0)
    def _():
        e_copy(-1).wait_send()

    @pl.when(moves)
    def _():
        e_copy(0).wait_send()
        for lr in range(2):
            a_copy(lr, 0).wait_send()

    for side in range(2):
        @pl.when(goes[side])
        def _():
            for lr in range(2):
                for j in range(8):
                    x_copy(lr, j, side).wait_send()
                for way in range(2):
                    y_copy(lr, way, 1 - 2 * side).wait_send()


def on_device(left_seeds, right_seeds, site_types, levels):
    dma = pltpu.SemaphoreType.DMA
    return pl.pallas_call(
        functools.partial(kernel, 1.0 / math.sqrt(512 * 1024)),
        out_shape=jax.ShapeDtypeStruct((32, 16), F32),
        in_specs=[pl.BlockSpec(memory_space=pl.ANY)] * 3 + [pl.BlockSpec(memory_space=pltpu.SMEM)],
        out_specs=pl.BlockSpec(memory_space=pltpu.VMEM),
        scratch_shapes=[
            pltpu.VMEM((2, 2, 32, 1024), F32),
            pltpu.VMEM((32, 1024), jnp.int32),
            pltpu.VMEM((2, 8, 2, 32, LANES), F32),
            pltpu.VMEM((3, 32, LANES), F32),
            pltpu.VMEM((3, 2, 8, 2, 32, LANES), F32),
            pltpu.VMEM((3, 2, 2, 8, 8, LANES), F32),
            pltpu.VMEM((3, 3, 32, LANES), F32),
            pltpu.VMEM((2, 2, 8, 8, LANES), F32),
            pltpu.VMEM((2, 96 + 2 * PAD, 2, 8, LANES), F32),
            pltpu.VMEM((96 + 2 * PAD, 2, 8, LANES), F32),
            pltpu.VMEM((2, 32, 256, LANES), F32),
            pltpu.VMEM((16, 2, 256, 256), BF16),
            pltpu.VMEM((256, 256), F32),
            pltpu.VMEM((16, 16, 256), F32),
            pltpu.VMEM((256, LANES), F32),
            pltpu.VMEM((8, 32, LANES), F32),
            dma((3,)),
            dma((2, 8)), dma((2, 8)), dma((2,)),
            dma((2, 2, 8)), dma((2, 2, 8)),
            dma((2, 2, 3)), dma((2, 2, 3)),
            dma((3,)), dma((3,)),
            dma((16,)), dma((16,)), dma((8,)), dma((8,)),
        ],
        compiler_params=pltpu.CompilerParams(
            collective_id=0, has_side_effects=True, vmem_limit_bytes=60 << 20),
    )(left_seeds, right_seeds, site_types, levels)


def solution(mesh):
    return jax.shard_map(
        on_device,
        mesh=mesh,
        in_specs=(P("mom", None, "site", None), P("mom", None, "site", None), P("site", None), P()),
        out_specs=P("mom", "site"),
        check_vma=False,
    )
```

```python
import functools
import math

import jax
import jax.numpy as jnp
from jax import lax
from jax.experimental import pallas as pl
from jax.experimental.pallas import tpu as pltpu
from jax.sharding import PartitionSpec as P

MB = 32
HOP = 2.0 / 4.2
HOP2 = HOP * HOP
MESH = pl.DeviceIdType.MESH
F32 = jnp.float32
BF16 = jnp.bfloat16
LANES = 128
HALF = 64
EDGE = 8
PAD = 4
PHASES = (1,) * 15


def snake(b):
    return jnp.where(b < 4, b, 11 - b)


def place(tile):
    return tile ^ (((tile >> 2) & 1) << 1)


def lanes_of(rows):
    return lax.broadcasted_iota(jnp.int32, (rows, LANES), 1)


def pieces(x):
    high = x.astype(BF16)
    rest = x - high.astype(F32)
    middle = rest.astype(BF16)
    low = (rest - middle.astype(F32)).astype(BF16)
    return jnp.concatenate([high, middle, low], axis=1)


def unzip(x):
    row = lax.broadcasted_iota(jnp.int32, (3 * LANES, LANES), 0) % LANES
    col = lax.broadcasted_iota(jnp.int32, (3 * LANES, LANES), 1)
    source = jnp.where(col < HALF, 2 * col, 2 * (col - HALF) + 1)
    matrix = jnp.where(row == source, 1.0, 0.0).astype(BF16)
    return jnp.dot(pieces(x), matrix, preferred_element_type=F32)


def spread_energy(ebuf, energy):
    lane = lanes_of(32)
    for tile in range(3):
        own, right, left = ebuf[tile, 1], ebuf[tile, 2], ebuf[tile, 0]
        turn = lambda x: pltpu.roll(x, HALF, 1)
        even = jnp.where(lane < HALF, own, jnp.where(lane < 96, turn(right), turn(left)))
        odd = jnp.where(lane < HALF, turn(own), jnp.where(lane < 96, right, left))
        for v, value in enumerate((even, odd)):
            for r in range(32):
                row = jnp.broadcast_to(value[r:r + 1, :], (8, LANES))
                energy[1, PAD + 32 * tile + r, v] = row
                energy[0, PAD + 32 * tile + r, v] = row * HOP2


def fill(lr, t, xbuf, ybuf, state):
    lane = lanes_of(8)
    inner = lane < HALF
    for tile in range(3):
        xs = xbuf.at[tile, lr].reshape(8 * 2 * 32, LANES)
        y0 = ybuf.at[tile, lr, 0].reshape(64, LANES)
        y1 = ybuf.at[tile, lr, 1].reshape(64, LANES)
        for r in range(8):
            low = y0[pl.ds(r, 8, stride=8), :]
            high = y1[pl.ds(r, 8, stride=8), :]
            for f in range(2):
                for g in range(4):
                    slot = f * 4 + g
                    row = 32 * tile + 8 * g + r
                    own = xs[pl.ds(f * 32 + 8 * g + r, 8, stride=64), :]
                    turn = lambda x, by: pltpu.roll(x, by % LANES, 1) if by % LANES else x
                    even = jnp.where(lane < 96, turn(high, HALF - EDGE * slot), turn(low, LANES - EDGE - EDGE * slot))
                    odd = jnp.where(lane < 96, turn(high, -EDGE * slot), turn(low, HALF - EDGE - EDGE * slot))
                    pair = (jnp.where(inner, own, even), jnp.where(inner, turn(own, HALF), odd))
                    for v in range(2):
                        new = pair[v] * HOP if f else pair[v]
                        if row == 31:
                            new = jnp.where(t == 0, 0.0, new)
                        if row == 64:
                            new = jnp.where(t == 15, 0.0, new)
                        state[f, PAD + row, v] = new


def step(lr, t, k, p, low, high, state, energy, arch):
    lane = lanes_of(8)
    load = lambda row: [state[p, PAD + row, v] for v in range(2)]
    below, here = load(low - 1), load(low)
    for row in range(low, high):
        above = load(row + 1)
        for v in range(2):
            across = pltpu.roll(here[1 - v], LANES - 1 if v else 1, 1) if row % 2 else here[1 - v]
            hops = above[v] + below[v] + across
            new = energy[p, PAD + row, v] * here[v] + (hops if p else hops * HOP2) - state[1 - p, PAD + row, v]
            if row == 31:
                new = jnp.where(t == 0, 0.0, new)
            if row == 64:
                new = jnp.where(t == 15, 0.0, new)
            state[1 - p, PAD + row, v] = new
        if 32 <= row < 64:
            keep(lr, lane, row, k, below, here, above, arch)
        below, here = here, above


def keep(lr, lane, row, k, below, here, above, arch):
    even, odd = [jnp.where(lr == 1, above[v] - below[v], here[v]) for v in range(2)]
    mine = jnp.where(lane < HALF, even, pltpu.roll(odd, HALF, 1))
    arch[lr, row - 32, pl.ds(pl.multiple_of(8 * k, 8), 8), :] = mine


def save(lr, k, p, state, arch):
    lane = lanes_of(8)
    for row in range(32, 64):
        load = lambda i: [state[p, PAD + row + i, v] for v in range(2)]
        keep(lr, lane, row, k, load(-1), load(0), load(1), arch)


def run(lr, t, state, energy, arch):
    save(lr, 0, 0, state, arch)
    k = 1
    for pairs in PHASES:
        first = k

        def double(i, unused):
            now = first + 2 * i
            step(lr, t, now, 1, first, 96 - first, state, energy, arch)
            step(lr, t, now + 1, 0, first + 1, 95 - first, state, energy, arch)
            return unused

        lax.fori_loop(0, pairs, double, 0)
        k += 2 * pairs
    save(lr, 31, 1, state, arch)


def halves(arch, lr, i):
    x = jnp.concatenate(
        [jnp.concatenate([arch[lr, 2 * i + n, pl.ds(q, 32, stride=8), :] for q in range(8)], axis=0)
         for n in range(2)], axis=1)
    high = x.astype(BF16)
    return high, (x - high.astype(F32)).astype(BF16)


def gram(arch, sums):
    sums[...] = jnp.zeros_like(sums)

    def product(a, c):
        return lax.dot_general(a, c, (((1,), (1,)), ((), ())), preferred_element_type=F32)

    def add(i, unused):
        lh, ll = halves(arch, 0, i)
        rh, rl = halves(arch, 1, i)
        sums[...] += product(rh, lh) + product(rh, ll) + product(rl, lh)
        return unused

    lax.fori_loop(0, 16, add, 0, unroll=4)


def kernel(scale, left_ref, right_ref, types_ref, levels_ref, out,
           raw, levels, types, seeds, levels_here, xbuf, ybuf, ebuf, pack, state, energy, arch, sums, got, turned,
           parts,
           in_sem, a_send, a_recv, own_sem, x_send, x_recv, y_send, y_recv, e_send, e_recv,
           s_send, s_recv, m_send, m_recv):
    t = lax.axis_index("site")
    b = lax.axis_index("mom")
    c = snake(b)
    mine = place(t)
    stays = mine == t
    moves = mine != t
    has_low = mine > 0
    has_high = mine < 15
    mom_right = snake(lax.rem(c + 1, 8))
    mom_left = snake(lax.rem(c + 7, 8))

    loads = [pltpu.make_async_copy(left_ref.at[0], raw.at[0], in_sem.at[0]),
             pltpu.make_async_copy(right_ref.at[0], raw.at[1], in_sem.at[1]),
             pltpu.make_async_copy(types_ref, types, in_sem.at[2]),
             pltpu.make_async_copy(levels_ref, levels, in_sem.at[3])]
    for load in loads:
        load.start()

    barrier = pltpu.get_barrier_semaphore()
    for j in range(1, 8):
        pl.semaphore_signal(barrier, inc=1, device_id=(t, lax.rem(b + j, 8)), device_id_type=MESH)
    for j in range(1, 16):
        pl.semaphore_signal(barrier, inc=1, device_id=(lax.rem(t + j, 16), b), device_id_type=MESH)
    for there, dt in ((has_low, -1), (has_high, 1)):
        @pl.when(there)
        def _():
            for q in (mom_left, mom_right):
                pl.semaphore_signal(barrier, inc=1, device_id=(place(mine + dt), q), device_id_type=MESH)

    @pl.when(moves)
    def _():
        for j in range(1, 8):
            pl.semaphore_signal(barrier, inc=1, device_id=(mine, lax.rem(b + j, 8)), device_id_type=MESH)

    def unzip_seeds(lr):
        x = jnp.concatenate(
            [raw[lr, :, :, LANES * i:LANES * i + LANES].reshape(64, LANES) for i in range(8)], axis=0)
        seeds[lr] = unzip(x).reshape(8, 2, 32, LANES)

    loads[0].wait()
    unzip_seeds(0)
    pl.semaphore_wait(
        barrier, 22 + jnp.where(has_low, 2, 0) + jnp.where(has_high, 2, 0) + jnp.where(moves, 7, 0))

    def a_copy(lr, j):
        q = lax.rem(b + j, 8)
        return pltpu.make_async_remote_copy(
            src_ref=seeds.at[lr, snake(q)], dst_ref=xbuf.at[1, lr, b],
            send_sem=a_send.at[lr, j], recv_sem=a_recv.at[lr, j],
            device_id=(mine, q), device_id_type=MESH)

    def a_arrival(lr, j):
        q = lax.rem(b + 8 - j, 8)
        return q, pltpu.make_async_remote_copy(
            src_ref=xbuf.at[1, lr, q], dst_ref=xbuf.at[1, lr, q],
            send_sem=a_send.at[lr, j], recv_sem=a_recv.at[lr, j],
            device_id=(mine, q), device_id_type=MESH)

    def own_copy(lr):
        return pltpu.make_async_copy(seeds.at[lr, c], xbuf.at[1, lr, b], own_sem.at[lr])

    def a_start(lr):
        for j in range(1, 8):
            a_copy(lr, j).start()

        @pl.when(stays)
        def _():
            own_copy(lr).start()

        @pl.when(moves)
        def _():
            a_copy(lr, 0).start()

    goes = (has_high, has_low)
    comes = (has_low, has_high)

    def e_copy(dt):
        return pltpu.make_async_remote_copy(
            src_ref=levels_here, dst_ref=ebuf.at[1 - dt],
            send_sem=e_send.at[1 - dt], recv_sem=e_recv.at[1 - dt],
            device_id=(place(t + dt), b), device_id_type=MESH)

    def e_keep():
        return pltpu.make_async_copy(levels_here, ebuf.at[1], e_send.at[1])

    def x_copy(lr, j, side):
        q = lax.rem(b + 8 - j, 8)
        return pltpu.make_async_remote_copy(
            src_ref=xbuf.at[1, lr, q], dst_ref=xbuf.at[2 * side, lr, q],
            send_sem=x_send.at[lr, side, j], recv_sem=x_recv.at[lr, side, j],
            device_id=(place(mine + 1 - 2 * side), b), device_id_type=MESH)

    def y_copy(lr, way, dt):
        q = mom_left if way else mom_right
        slot = 1 - dt
        return pltpu.make_async_remote_copy(
            src_ref=pack.at[lr, way], dst_ref=ybuf.at[slot, lr, way],
            send_sem=y_send.at[lr, way, slot], recv_sem=y_recv.at[lr, way, slot],
            device_id=(place(mine + dt), q), device_id_type=MESH)

    a_start(0)
    loads[1].wait()
    unzip_seeds(1)
    a_start(1)

    loads[2].wait()
    loads[3].wait()
    values = []
    for n in range(3):
        col = pl.multiple_of(lax.rem(c + 7 + n, 8) * LANES, LANES)
        kinds = types[:, pl.ds(col, LANES)]
        value = jnp.zeros((32, LANES), F32)
        for kind in range(4):
            value = jnp.where(kinds == kind, levels[kind], value)
        values.append(value)
    levels_here[...] = unzip(jnp.concatenate(values, axis=0)).reshape(3, 32, LANES)

    @pl.when(t < 15)
    def _():
        e_copy(1).start()

    @pl.when(t > 0)
    def _():
        e_copy(-1).start()

    @pl.when(moves)
    def _():
        e_copy(0).start()

    @pl.when(stays)
    def _():
        e_keep().start()

    lane = lanes_of(8)

    def forward(lr):
        for j in range(8):
            if j == 0:
                q = b

                @pl.when(stays)
                def _():
                    own_copy(lr).wait()

                @pl.when(moves)
                def _():
                    a_copy(lr, 0).wait_recv()
            else:
                q, arrival = a_arrival(lr, j)
                arrival.wait_recv()
            for side in range(2):
                @pl.when(goes[side])
                def _():
                    x_copy(lr, j, side).start()
            for way in range(2):
                packed = None
                for f in range(2):
                    for g in range(4):
                        slot = f * 4 + g
                        v = xbuf[1, lr, q, f, 8 * g:8 * g + 8, :]
                        source = 0 if way else HALF - EDGE
                        v = pltpu.roll(v, (EDGE * slot - source) % LANES, 1) if EDGE * slot != source else v
                        packed = v if packed is None else jnp.where(lane % HALF >= EDGE * slot, v, packed)
                pack[lr, way, q] = packed
        for way in range(2):
            y_copy(lr, way, 0).start()
            for side in range(2):
                @pl.when(goes[side])
                def _():
                    y_copy(lr, way, 1 - 2 * side).start()

    forward(0)
    forward(1)

    for side in range(2):
        @pl.when(comes[side])
        def _():
            e_copy(1 - 2 * side).wait_recv()

    @pl.when(moves)
    def _():
        e_copy(0).wait_recv()

    @pl.when(stays)
    def _():
        e_keep().wait()

    spread_energy(ebuf, energy)

    def side_of(lr, unused):
        for way in range(2):
            y_copy(lr, way, 0).wait_recv()
        for side in range(2):
            @pl.when(comes[side])
            def _():
                for j in range(8):
                    x_copy(lr, j, side).wait_recv()
                for way in range(2):
                    y_copy(lr, way, 1 - 2 * side).wait_recv()
        fill(lr, mine, xbuf, ybuf, state)
        run(lr, mine, state, energy, arch)
        return unused

    lax.fori_loop(0, 2, side_of, 0)
    gram(arch, sums)

    def s_copy(j):
        s = lax.rem(t + j, 16)
        return pltpu.make_async_remote_copy(
            src_ref=sums.at[pl.ds(pl.multiple_of(16 * s, 16), 16), :], dst_ref=got.at[j],
            send_sem=s_send.at[j], recv_sem=s_recv.at[j], device_id=(s, b), device_id_type=MESH)

    for j in range(1, 16):
        s_copy(j).start()
    total = sums[pl.ds(pl.multiple_of(16 * t, 16), 16), :]
    for j in range(1, 16):
        s_copy(j).wait_recv()
        total = total + got[j]
    for q in range(8):
        column = LANES * (q // 4)
        first, second = total[0:8, column:column + LANES], total[8:16, column:column + LANES]
        shift = 32 * (q % 4)
        turn = lambda x, by: pltpu.roll(x, by % LANES, 1) if by % LANES else x
        turned[q] = jnp.where(lane < 32, turn(first, -shift), turn(second, 32 - shift))

    def m_copy(j):
        q = lax.rem(b + j, 8)
        return pltpu.make_async_remote_copy(
            src_ref=turned.at[q], dst_ref=parts.at[j],
            send_sem=m_send.at[j], recv_sem=m_recv.at[j], device_id=(t, q), device_id_type=MESH)

    for j in range(1, 8):
        m_copy(j).start()
    final = turned[b]
    for j in range(1, 8):
        m_copy(j).wait_recv()
        final = final + parts[j]
    block = jnp.transpose(final)
    block = jnp.concatenate([block[0:32], block[32:64]], axis=1)
    odds = (lax.broadcasted_iota(jnp.int32, (32, 16), 0) % 2) + (lax.broadcasted_iota(jnp.int32, (32, 16), 1) % 2)
    out[...] = block * jnp.where(odds == 0, scale, jnp.where(odds == 1, scale / HOP, scale / HOP2))

    for j in range(1, 16):
        s_copy(j).wait_send()
    for j in range(1, 8):
        m_copy(j).wait_send()
    for lr in range(2):
        for j in range(1, 8):
            a_copy(lr, j).wait_send()
        for way in range(2):
            y_copy(lr, way, 0).wait_send()

    @pl.when(t < 15)
    def _():
        e_copy(1).wait_send()

    @pl.when(t > 0)
    def _():
        e_copy(-1).wait_send()

    @pl.when(moves)
    def _():
        e_copy(0).wait_send()
        for lr in range(2):
            a_copy(lr, 0).wait_send()

    for side in range(2):
        @pl.when(goes[side])
        def _():
            for lr in range(2):
                for j in range(8):
                    x_copy(lr, j, side).wait_send()
                for way in range(2):
                    y_copy(lr, way, 1 - 2 * side).wait_send()


def on_device(left_seeds, right_seeds, site_types, levels):
    dma = pltpu.SemaphoreType.DMA
    return pl.pallas_call(
        functools.partial(kernel, 1.0 / math.sqrt(512 * 1024)),
        out_shape=jax.ShapeDtypeStruct((32, 16), F32),
        in_specs=[pl.BlockSpec(memory_space=pl.ANY)] * 4,
        out_specs=pl.BlockSpec(memory_space=pltpu.VMEM),
        scratch_shapes=[
            pltpu.VMEM((2, 2, 32, 1024), F32),
            pltpu.SMEM((4,), F32),
            pltpu.VMEM((32, 1024), jnp.int32),
            pltpu.VMEM((2, 8, 2, 32, LANES), F32),
            pltpu.VMEM((3, 32, LANES), F32),
            pltpu.VMEM((3, 2, 8, 2, 32, LANES), F32),
            pltpu.VMEM((3, 2, 2, 8, 8, LANES), F32),
            pltpu.VMEM((3, 3, 32, LANES), F32),
            pltpu.VMEM((2, 2, 8, 8, LANES), F32),
            pltpu.VMEM((2, 96 + 2 * PAD, 2, 8, LANES), F32),
            pltpu.VMEM((2, 96 + 2 * PAD, 2, 8, LANES), F32),
            pltpu.VMEM((2, 32, 256, LANES), F32),
            pltpu.VMEM((256, 256), F32),
            pltpu.VMEM((16, 16, 256), F32),
            pltpu.VMEM((8, 8, LANES), F32),
            pltpu.VMEM((8, 8, LANES), F32),
            dma((4,)),
            dma((2, 8)), dma((2, 8)), dma((2,)),
            dma((2, 2, 8)), dma((2, 2, 8)),
            dma((2, 2, 3)), dma((2, 2, 3)),
            dma((3,)), dma((3,)),
            dma((16,)), dma((16,)), dma((8,)), dma((8,)),
        ],
        compiler_params=pltpu.CompilerParams(
            collective_id=0, has_side_effects=True, vmem_limit_bytes=60 << 20),
    )(left_seeds, right_seeds, site_types, levels)


def solution(mesh):
    return jax.shard_map(
        on_device,
        mesh=mesh,
        in_specs=(P("mom", None, "site", None), P("mom", None, "site", None), P("site", None), P()),
        out_specs=P("mom", "site"),
        check_vma=False,
    )
```

```python
import functools
import math

import jax
import jax.numpy as jnp
from jax import lax
from jax.experimental import pallas as pl
from jax.experimental.pallas import tpu as pltpu
from jax.sharding import PartitionSpec as P

MB = 32
HOP = 2.0 / 4.2
HOP2 = HOP * HOP
MESH = pl.DeviceIdType.MESH
F32 = jnp.float32
BF16 = jnp.bfloat16
LANES = 128
HALF = 64
EDGE = 8
PAD = 4
PHASES = (1,) * 15


def snake(b):
    return jnp.where(b < 4, b, 11 - b)


def place(tile):
    return tile ^ (((tile >> 2) & 1) << 1)


def lanes_of(rows):
    return lax.broadcasted_iota(jnp.int32, (rows, LANES), 1)


def pieces(x):
    high = x.astype(BF16)
    rest = x - high.astype(F32)
    middle = rest.astype(BF16)
    low = (rest - middle.astype(F32)).astype(BF16)
    return jnp.concatenate([high, middle, low], axis=1)


def unzip(x):
    row = lax.broadcasted_iota(jnp.int32, (3 * LANES, LANES), 0) % LANES
    col = lax.broadcasted_iota(jnp.int32, (3 * LANES, LANES), 1)
    source = jnp.where(col < HALF, 2 * col, 2 * (col - HALF) + 1)
    matrix = jnp.where(row == source, 1.0, 0.0).astype(BF16)
    return jnp.dot(pieces(x), matrix, preferred_element_type=F32)


def spread_energy(ebuf, energy):
    lane = lanes_of(32)
    for tile in range(3):
        own, right, left = ebuf[tile, 1], ebuf[tile, 2], ebuf[tile, 0]
        turn = lambda x: pltpu.roll(x, HALF, 1)
        even = jnp.where(lane < HALF, own, jnp.where(lane < 96, turn(right), turn(left)))
        odd = jnp.where(lane < HALF, turn(own), jnp.where(lane < 96, right, left))
        for v, value in enumerate((even, odd)):
            for r in range(32):
                row = jnp.broadcast_to(value[r:r + 1, :], (8, LANES))
                energy[1, PAD + 32 * tile + r, v] = row
                energy[0, PAD + 32 * tile + r, v] = row * HOP2


def fill(lr, t, xbuf, ybuf, state):
    lane = lanes_of(8)
    inner = lane < HALF
    for tile in range(3):
        xs = xbuf.at[tile, lr].reshape(8 * 2 * 32, LANES)
        y0 = ybuf.at[tile, lr, 0].reshape(64, LANES)
        y1 = ybuf.at[tile, lr, 1].reshape(64, LANES)
        for r in range(8):
            low = y0[pl.ds(r, 8, stride=8), :]
            high = y1[pl.ds(r, 8, stride=8), :]
            for f in range(2):
                for g in range(4):
                    slot = f * 4 + g
                    row = 32 * tile + 8 * g + r
                    own = xs[pl.ds(f * 32 + 8 * g + r, 8, stride=64), :]
                    turn = lambda x, by: pltpu.roll(x, by % LANES, 1) if by % LANES else x
                    even = jnp.where(lane < 96, turn(high, HALF - EDGE * slot), turn(low, LANES - EDGE - EDGE * slot))
                    odd = jnp.where(lane < 96, turn(high, -EDGE * slot), turn(low, HALF - EDGE - EDGE * slot))
                    pair = (jnp.where(inner, own, even), jnp.where(inner, turn(own, HALF), odd))
                    for v in range(2):
                        new = pair[v] * HOP if f else pair[v]
                        if row == 31:
                            new = jnp.where(t == 0, 0.0, new)
                        if row == 64:
                            new = jnp.where(t == 15, 0.0, new)
                        state[f, PAD + row, v] = new


def step(lr, t, k, p, low, high, state, energy, arch):
    lane = lanes_of(8)
    load = lambda row: [state[p, PAD + row, v] for v in range(2)]
    below, here = load(low - 1), load(low)
    for row in range(low, high):
        above = load(row + 1)
        for v in range(2):
            across = pltpu.roll(here[1 - v], LANES - 1 if v else 1, 1) if row % 2 else here[1 - v]
            hops = above[v] + below[v] + across
            new = energy[p, PAD + row, v] * here[v] + (hops if p else hops * HOP2) - state[1 - p, PAD + row, v]
            if row == 31:
                new = jnp.where(t == 0, 0.0, new)
            if row == 64:
                new = jnp.where(t == 15, 0.0, new)
            state[1 - p, PAD + row, v] = new
        if 32 <= row < 64:
            keep(lr, lane, row, k, below, here, above, arch)
        below, here = here, above


def keep(lr, lane, row, k, below, here, above, arch):
    even, odd = [jnp.where(lr == 1, above[v] - below[v], here[v]) for v in range(2)]
    mine = jnp.where(lane < HALF, even, pltpu.roll(odd, HALF, 1))
    arch[lr, row - 32, pl.ds(pl.multiple_of(8 * k, 8), 8), :] = mine


def save(lr, k, p, state, arch):
    lane = lanes_of(8)
    for row in range(32, 64):
        load = lambda i: [state[p, PAD + row + i, v] for v in range(2)]
        keep(lr, lane, row, k, load(-1), load(0), load(1), arch)


def run(lr, t, state, energy, arch):
    save(lr, 0, 0, state, arch)
    k = 1
    for pairs in PHASES:
        first = k

        def double(i, unused):
            now = first + 2 * i
            step(lr, t, now, 1, first, 96 - first, state, energy, arch)
            step(lr, t, now + 1, 0, first + 1, 95 - first, state, energy, arch)
            return unused

        lax.fori_loop(0, pairs, double, 0)
        k += 2 * pairs
    save(lr, 31, 1, state, arch)


def halves(arch, lr, i):
    x = jnp.concatenate(
        [jnp.concatenate([arch[lr, 2 * i + n, pl.ds(q, 32, stride=8), :] for q in range(8)], axis=0)
         for n in range(2)], axis=1)
    high = x.astype(BF16)
    return high, (x - high.astype(F32)).astype(BF16)


def gram(arch, sums):
    sums[...] = jnp.zeros_like(sums)

    def product(a, c):
        return lax.dot_general(a, c, (((1,), (1,)), ((), ())), preferred_element_type=F32)

    def add(i, unused):
        lh, ll = halves(arch, 0, i)
        rh, rl = halves(arch, 1, i)
        sums[...] += product(rh, lh) + product(rh, ll) + product(rl, lh)
        return unused

    lax.fori_loop(0, 16, add, 0, unroll=4)


def kernel(scale, left_ref, right_ref, types_ref, levels_ref, out,
           raw, levels, types, seeds, levels_here, xbuf, ybuf, ebuf, pack, state, energy, arch, sums, got, turned,
           parts,
           in_sem, a_send, a_recv, own_sem, x_send, x_recv, y_send, y_recv, e_send, e_recv,
           s_send, s_recv, m_send, m_recv):
    t = lax.axis_index("site")
    b = lax.axis_index("mom")
    c = snake(b)
    mine = place(t)
    stays = mine == t
    moves = mine != t
    has_low = mine > 0
    has_high = mine < 15
    mom_right = snake(lax.rem(c + 1, 8))
    mom_left = snake(lax.rem(c + 7, 8))

    loads = [pltpu.make_async_copy(left_ref.at[0], raw.at[0], in_sem.at[0]),
             pltpu.make_async_copy(right_ref.at[0], raw.at[1], in_sem.at[1]),
             pltpu.make_async_copy(types_ref, types, in_sem.at[2]),
             pltpu.make_async_copy(levels_ref, levels, in_sem.at[3])]
    for load in loads:
        load.start()

    barrier = pltpu.get_barrier_semaphore()
    for j in range(1, 8):
        pl.semaphore_signal(barrier, inc=1, device_id=(t, lax.rem(b + j, 8)), device_id_type=MESH)
    for j in range(1, 16):
        pl.semaphore_signal(barrier, inc=1, device_id=(lax.rem(t + j, 16), b), device_id_type=MESH)
    for there, dt in ((has_low, -1), (has_high, 1)):
        @pl.when(there)
        def _():
            for q in (mom_left, mom_right):
                pl.semaphore_signal(barrier, inc=1, device_id=(place(mine + dt), q), device_id_type=MESH)

    @pl.when(moves)
    def _():
        for j in range(1, 8):
            pl.semaphore_signal(barrier, inc=1, device_id=(mine, lax.rem(b + j, 8)), device_id_type=MESH)

    def unzip_seeds(lr):
        x = jnp.concatenate(
            [raw[lr, :, :, LANES * i:LANES * i + LANES].reshape(64, LANES) for i in range(8)], axis=0)
        seeds[lr] = unzip(x).reshape(8, 2, 32, LANES)

    loads[0].wait()
    unzip_seeds(0)
    pl.semaphore_wait(
        barrier, 22 + jnp.where(has_low, 2, 0) + jnp.where(has_high, 2, 0) + jnp.where(moves, 7, 0))

    def a_copy(lr, j):
        q = lax.rem(b + j, 8)
        return pltpu.make_async_remote_copy(
            src_ref=seeds.at[lr, snake(q)], dst_ref=xbuf.at[1, lr, b],
            send_sem=a_send.at[lr, j], recv_sem=a_recv.at[lr, j],
            device_id=(mine, q), device_id_type=MESH)

    def a_arrival(lr, j):
        q = lax.rem(b + 8 - j, 8)
        return q, pltpu.make_async_remote_copy(
            src_ref=xbuf.at[1, lr, q], dst_ref=xbuf.at[1, lr, q],
            send_sem=a_send.at[lr, j], recv_sem=a_recv.at[lr, j],
            device_id=(mine, q), device_id_type=MESH)

    def own_copy(lr):
        return pltpu.make_async_copy(seeds.at[lr, c], xbuf.at[1, lr, b], own_sem.at[lr])

    def a_start(lr):
        for j in range(1, 8):
            a_copy(lr, j).start()

        @pl.when(stays)
        def _():
            own_copy(lr).start()

        @pl.when(moves)
        def _():
            a_copy(lr, 0).start()

    goes = (has_high, has_low)
    comes = (has_low, has_high)

    def e_copy(dt):
        return pltpu.make_async_remote_copy(
            src_ref=levels_here, dst_ref=ebuf.at[1 - dt],
            send_sem=e_send.at[1 - dt], recv_sem=e_recv.at[1 - dt],
            device_id=(place(t + dt), b), device_id_type=MESH)

    def e_keep():
        return pltpu.make_async_copy(levels_here, ebuf.at[1], e_send.at[1])

    def x_copy(lr, j, side):
        q = lax.rem(b + 8 - j, 8)
        return pltpu.make_async_remote_copy(
            src_ref=xbuf.at[1, lr, q], dst_ref=xbuf.at[2 * side, lr, q],
            send_sem=x_send.at[lr, side, j], recv_sem=x_recv.at[lr, side, j],
            device_id=(place(mine + 1 - 2 * side), b), device_id_type=MESH)

    def y_copy(lr, way, dt):
        q = mom_left if way else mom_right
        slot = 1 - dt
        return pltpu.make_async_remote_copy(
            src_ref=pack.at[lr, way], dst_ref=ybuf.at[slot, lr, way],
            send_sem=y_send.at[lr, way, slot], recv_sem=y_recv.at[lr, way, slot],
            device_id=(place(mine + dt), q), device_id_type=MESH)

    a_start(0)
    loads[1].wait()
    unzip_seeds(1)
    a_start(1)

    loads[2].wait()
    loads[3].wait()
    values = []
    for n in range(3):
        col = pl.multiple_of(lax.rem(c + 7 + n, 8) * LANES, LANES)
        kinds = types[:, pl.ds(col, LANES)]
        value = jnp.zeros((32, LANES), F32)
        for kind in range(4):
            value = jnp.where(kinds == kind, levels[kind], value)
        values.append(value)
    levels_here[...] = unzip(jnp.concatenate(values, axis=0)).reshape(3, 32, LANES)

    @pl.when(t < 15)
    def _():
        e_copy(1).start()

    @pl.when(t > 0)
    def _():
        e_copy(-1).start()

    @pl.when(moves)
    def _():
        e_copy(0).start()

    @pl.when(stays)
    def _():
        e_keep().start()

    lane = lanes_of(8)

    def forward(lr):
        for j in range(8):
            if j == 0:
                q = b

                @pl.when(stays)
                def _():
                    own_copy(lr).wait()

                @pl.when(moves)
                def _():
                    a_copy(lr, 0).wait_recv()
            else:
                q, arrival = a_arrival(lr, j)
                arrival.wait_recv()
            for side in range(2):
                @pl.when(goes[side])
                def _():
                    x_copy(lr, j, side).start()
            for way in range(2):
                packed = None
                for f in range(2):
                    for g in range(4):
                        slot = f * 4 + g
                        v = xbuf[1, lr, q, f, 8 * g:8 * g + 8, :]
                        source = 0 if way else HALF - EDGE
                        v = pltpu.roll(v, (EDGE * slot - source) % LANES, 1) if EDGE * slot != source else v
                        packed = v if packed is None else jnp.where(lane % HALF >= EDGE * slot, v, packed)
                pack[lr, way, q] = packed
        for way in range(2):
            y_copy(lr, way, 0).start()
            for side in range(2):
                @pl.when(goes[side])
                def _():
                    y_copy(lr, way, 1 - 2 * side).start()

    forward(0)
    forward(1)

    for side in range(2):
        @pl.when(comes[side])
        def _():
            e_copy(1 - 2 * side).wait_recv()

    @pl.when(moves)
    def _():
        e_copy(0).wait_recv()

    @pl.when(stays)
    def _():
        e_keep().wait()

    spread_energy(ebuf, energy)

    def side_of(lr, unused):
        for way in range(2):
            y_copy(lr, way, 0).wait_recv()
        for side in range(2):
            @pl.when(comes[side])
            def _():
                for j in range(8):
                    x_copy(lr, j, side).wait_recv()
                for way in range(2):
                    y_copy(lr, way, 1 - 2 * side).wait_recv()
        fill(lr, mine, xbuf, ybuf, state)
        run(lr, mine, state, energy, arch)
        return unused

    lax.fori_loop(0, 2, side_of, 0)
    gram(arch, sums)

    def s_copy(j):
        s = lax.rem(t + j, 16)
        return pltpu.make_async_remote_copy(
            src_ref=sums.at[pl.ds(pl.multiple_of(16 * s, 16), 16), :], dst_ref=got.at[j],
            send_sem=s_send.at[j], recv_sem=s_recv.at[j], device_id=(s, b), device_id_type=MESH)

    for j in range(1, 16):
        s_copy(j).start()
    total = sums[pl.ds(pl.multiple_of(16 * t, 16), 16), :]
    for j in range(1, 16):
        s_copy(j).wait_recv()
        total = total + got[j]
    for q in range(8):
        column = LANES * (q // 4)
        first, second = total[0:8, column:column + LANES], total[8:16, column:column + LANES]
        shift = 32 * (q % 4)
        turn = lambda x, by: pltpu.roll(x, by % LANES, 1) if by % LANES else x
        turned[q] = jnp.where(lane < 32, turn(first, -shift), turn(second, 32 - shift))

    def m_copy(j):
        q = lax.rem(b + j, 8)
        return pltpu.make_async_remote_copy(
            src_ref=turned.at[q], dst_ref=parts.at[j],
            send_sem=m_send.at[j], recv_sem=m_recv.at[j], device_id=(t, q), device_id_type=MESH)

    for j in range(1, 8):
        m_copy(j).start()
    final = turned[b]
    for j in range(1, 8):
        m_copy(j).wait_recv()
        final = final + parts[j]
    block = jnp.transpose(final)
    block = jnp.concatenate([block[0:32], block[32:64]], axis=1)
    odds = (lax.broadcasted_iota(jnp.int32, (32, 16), 0) % 2) + (lax.broadcasted_iota(jnp.int32, (32, 16), 1) % 2)
    out[...] = block * jnp.where(odds == 0, scale, jnp.where(odds == 1, scale / HOP, scale / HOP2))

    for j in range(1, 16):
        s_copy(j).wait_send()
    for j in range(1, 8):
        m_copy(j).wait_send()
    for lr in range(2):
        for j in range(1, 8):
            a_copy(lr, j).wait_send()
        for way in range(2):
            y_copy(lr, way, 0).wait_send()

    @pl.when(t < 15)
    def _():
        e_copy(1).wait_send()

    @pl.when(t > 0)
    def _():
        e_copy(-1).wait_send()

    @pl.when(moves)
    def _():
        e_copy(0).wait_send()
        for lr in range(2):
            a_copy(lr, 0).wait_send()

    for side in range(2):
        @pl.when(goes[side])
        def _():
            for lr in range(2):
                for j in range(8):
                    x_copy(lr, j, side).wait_send()
                for way in range(2):
                    y_copy(lr, way, 1 - 2 * side).wait_send()


def on_device(left_seeds, right_seeds, site_types, levels):
    dma = pltpu.SemaphoreType.DMA
    return pl.pallas_call(
        functools.partial(kernel, 1.0 / math.sqrt(512 * 1024)),
        out_shape=jax.ShapeDtypeStruct((32, 16), F32),
        in_specs=[pl.BlockSpec(memory_space=pl.ANY)] * 4,
        out_specs=pl.BlockSpec(memory_space=pltpu.VMEM),
        scratch_shapes=[
            pltpu.VMEM((2, 2, 32, 1024), F32),
            pltpu.SMEM((4,), F32),
            pltpu.VMEM((32, 1024), jnp.int32),
            pltpu.VMEM((2, 8, 2, 32, LANES), F32),
            pltpu.VMEM((3, 32, LANES), F32),
            pltpu.VMEM((3, 2, 8, 2, 32, LANES), F32),
            pltpu.VMEM((3, 2, 2, 8, 8, LANES), F32),
            pltpu.VMEM((3, 3, 32, LANES), F32),
            pltpu.VMEM((2, 2, 8, 8, LANES), F32),
            pltpu.VMEM((2, 96 + 2 * PAD, 2, 8, LANES), F32),
            pltpu.VMEM((2, 96 + 2 * PAD, 2, 8, LANES), F32),
            pltpu.VMEM((2, 32, 256, LANES), F32),
            pltpu.VMEM((256, 256), F32),
            pltpu.VMEM((16, 16, 256), F32),
            pltpu.VMEM((8, 8, LANES), F32),
            pltpu.VMEM((8, 8, LANES), F32),
            dma((4,)),
            dma((2, 8)), dma((2, 8)), dma((2,)),
            dma((2, 2, 8)), dma((2, 2, 8)),
            dma((2, 2, 3)), dma((2, 2, 3)),
            dma((3,)), dma((3,)),
            dma((16,)), dma((16,)), dma((8,)), dma((8,)),
        ],
        compiler_params=pltpu.CompilerParams(
            collective_id=0, has_side_effects=True, vmem_limit_bytes=539 * (1 << 20) // 10),
    )(left_seeds, right_seeds, site_types, levels)


def solution(mesh):
    return jax.shard_map(
        on_device,
        mesh=mesh,
        in_specs=(P("mom", None, "site", None), P("mom", None, "site", None), P("site", None), P()),
        out_specs=P("mom", "site"),
        check_vma=False,
    )
```
